512 devices in a mesh: tm: 32 (over z_lo, y, core), space: 16 (over x, z_hi).
Axes of the slice: x: 4, y: 4, z: 16 (z_hi: 4, z_lo: 4; z = z_hi * 4 + z_lo), core: 2. Of those that a mesh axis runs over, the one named last changes fastest.
Arguments:
- evecs: float32 [32, 2, 12288, 256], P('tm', None, 'space'), may hold values from -0.0546875 to 0.0546875
- solutions: float32 [32, 2, 12288, 512], P('tm', None, 'space'), may hold values from -6 to 6
- sink_time_weight: float32 [32, 32], P(None, 'tm'), may hold values from 0.1 to 1
- noise_source_vector: float32 [32, 2, 4, 256], P('tm'), may hold values from -6 to 6
- probe: float32 [32, 2, 4, 256], P('tm'), may hold values from -6 to 6
- dilution_spin_index: int32 [32, 4], P('tm'), may hold values from 0 to 3
- dilution_lace_index: int32 [32, 4], P('tm'), may hold values from 0 to 7
Outputs:
- smeared: float32 [32, 2, 16, 12288], P('tm', None, None, 'space')
The draws below stay inside these ranges and needn't reach their ends.
All inputs are finite; a program needn't handle non-finite values.
Results may differ from the reference program's by a relative error of at most 0.000071.
Values sent between devices are 32-bit elements; how exact they have to be, the bound alone decides.
A program may use at most 64 MiB of HBM per device.

```python
import math
import jax
import jax.numpy as jnp
from jax import lax

EIGEN_COUNT = 256
DILUTION_COUNT = 4
SPIN_COUNT = 4
LACE_CLASSES = 8
TIME_SLICES = 32
ROWS = 12288
COLS = 512


def plant(drawn, key, low, high):
    index_at = [jax.random.randint(jax.random.fold_in(key, axis), (), 0, length) for axis, length in enumerate(drawn.shape)]
    main_axis = drawn.shape.index(max(drawn.shape))
    next_to = index_at[:main_axis] + [(index_at[main_axis] + 1) % drawn.shape[main_axis]] + index_at[main_axis + 1:]
    return drawn.at[tuple(index_at)].set(low).at[tuple(next_to)].set(high)


def shard_levels(rng, dims, cuts, low, top_value):
    loudness, own = 1.0, jax.random.fold_in(rng, 6)
    for position, shards_of in cuts:
        draws = jnp.exp(jax.random.uniform(jax.random.fold_in(own, position), (shards_of,), jnp.float32, low / len(cuts), top_value / len(cuts)))
        loudness = loudness * jnp.repeat(draws, dims[position] // shards_of).reshape([-1 if axis == position else 1 for axis in range(len(dims))])
    return loudness


def centred(stream_key, extent, deviation, limit, cuts=(), held_as=jnp.bfloat16):
    level = shard_levels(stream_key, extent, cuts, -0.22, 0.18) if cuts else 1.0
    values = jax.random.normal(stream_key, extent, jnp.float32) * deviation * level
    return jnp.minimum(jnp.maximum(values, -limit), limit).astype(held_as)


def setup_inputs(seed: int = 0) -> dict:
    key_list = jax.random.split(jax.random.key(seed), 8)
    return {
        "evecs": centred(key_list[0], (TIME_SLICES, 2, ROWS, EIGEN_COUNT), ROWS ** -0.5, 0.0546875, ((0, 32), (2, 16)), jnp.float32),
        "solutions": centred(key_list[1], (TIME_SLICES, 2, ROWS, COLS), 1.0, 6.0, ((0, 32), (2, 16)), jnp.float32),
        "sink_time_weight": jnp.clip(jnp.exp(math.log(1.0) - 2.3025851 * jax.random.uniform(key_list[2], (TIME_SLICES, TIME_SLICES), jnp.float32) ** shard_levels(key_list[2], (TIME_SLICES, TIME_SLICES), ((1, 32),), -0.2, 0.2)), 0.1, 1.0),
        "noise_source_vector": centred(key_list[3], (TIME_SLICES, 2, SPIN_COUNT, EIGEN_COUNT), 1.0, 6.0, ((0, 32),), jnp.float32),
        "probe": centred(key_list[4], (TIME_SLICES, 2, SPIN_COUNT, EIGEN_COUNT), 1.0, 6.0, ((0, 32),), jnp.float32),
        "dilution_spin_index": plant(jax.random.randint(key_list[5], (TIME_SLICES, DILUTION_COUNT), 0, SPIN_COUNT), jax.random.fold_in(key_list[5], 1), 0, SPIN_COUNT - 1).astype(jnp.int32),
        "dilution_lace_index": plant(jax.random.randint(key_list[6], (TIME_SLICES, DILUTION_COUNT), 0, LACE_CLASSES), jax.random.fold_in(key_list[6], 1), 0, LACE_CLASSES - 1).astype(jnp.int32),
    }


def project(pieces):
    vreal, vimag, preal, pimag = pieces
    hp = lax.Precision.HIGHEST
    real = jnp.dot(vreal.T, preal, precision=hp, preferred_element_type=jnp.float32) + jnp.dot(vimag.T, pimag, precision=hp, preferred_element_type=jnp.float32)
    imag = jnp.dot(vreal.T, pimag, precision=hp, preferred_element_type=jnp.float32) - jnp.dot(vimag.T, preal, precision=hp, preferred_element_type=jnp.float32)
    return jnp.stack([real, imag])


def reference(evecs, solutions, sink_time_weight, noise_source_vector, probe, dilution_spin_index, dilution_lace_index):
    hp = lax.Precision.HIGHEST
    mode_coefficients = lax.map(project, (evecs[:, 0], evecs[:, 1], solutions[:, 0], solutions[:, 1]))
    mode_coefficients = mode_coefficients.reshape(TIME_SLICES, 2, EIGEN_COUNT, TIME_SLICES, DILUTION_COUNT * SPIN_COUNT)
    summed_result = jnp.einsum("tcnuj,tu->ucnj", mode_coefficients, sink_time_weight, precision=hp)
    summed_result = summed_result.reshape(TIME_SLICES, 2, EIGEN_COUNT, DILUTION_COUNT, SPIN_COUNT)
    vector_lanes = jnp.arange(EIGEN_COUNT, dtype=jnp.int32) % LACE_CLASSES
    lace_matches = (vector_lanes[None, None, :] == dilution_lace_index[:, :, None]).astype(jnp.float32)
    spin_matches = (jnp.arange(SPIN_COUNT, dtype=jnp.int32)[None, None, :] == dilution_spin_index[:, :, None]).astype(jnp.float32)
    ereal, eimag = noise_source_vector[:, 0], noise_source_vector[:, 1]
    preal, pimag = probe[:, 0], probe[:, 1]
    prod_real = ereal * preal + eimag * pimag
    prod_imag = ereal * pimag - eimag * preal
    w_real = jnp.einsum("tkm,tsm->tks", lace_matches, prod_real, precision=hp) * spin_matches
    w_imag = jnp.einsum("tkm,tsm->tks", lace_matches, prod_imag, precision=hp) * spin_matches
    y_real, y_imag = summed_result[:, 0], summed_result[:, 1]
    z_real = jnp.einsum("tnka,tks->tnas", y_real, w_real, precision=hp) - jnp.einsum("tnka,tks->tnas", y_imag, w_imag, precision=hp)
    z_imag = jnp.einsum("tnka,tks->tnas", y_real, w_imag, precision=hp) + jnp.einsum("tnka,tks->tnas", y_imag, w_real, precision=hp)
    z_real = z_real.reshape(TIME_SLICES, EIGEN_COUNT, SPIN_COUNT * SPIN_COUNT)
    z_imag = z_imag.reshape(TIME_SLICES, EIGEN_COUNT, SPIN_COUNT * SPIN_COUNT)
    vreal, vimag = evecs[:, 0], evecs[:, 1]
    f_real = jnp.einsum("trn,tnq->tqr", vreal, z_real, precision=hp) - jnp.einsum("trn,tnq->tqr", vimag, z_imag, precision=hp)
    f_imag = jnp.einsum("trn,tnq->tqr", vreal, z_imag, precision=hp) + jnp.einsum("trn,tnq->tqr", vimag, z_real, precision=hp)
    return jnp.stack([f_real, f_imag], axis=1)
```

```python
import jax
import jax.numpy as jnp
from jax import lax
from jax.experimental import pallas as pl
from jax.experimental.pallas import tpu as pltpu
from jax.sharding import PartitionSpec as P

F32 = jnp.float32
BF16 = jnp.bfloat16
MESH = pl.DeviceIdType.MESH

NX, NY, NC, NZH, NZL = 4, 4, 2, 4, 4
MODES = 256
HALF = 128
ROWS = 768
BLOCK = 16
LACE_CLASSES = 8
CHUNK_ZL = ((0, 3), (1, 2))


def ring(d, n):
    return min(d, n - d)


PLANE = sorted(
    [(dx, dy, dc) for dx in range(NX) for dy in range(NY) for dc in range(NC) if (dx, dy, dc) != (0, 0, 0)],
    key=lambda o: -(ring(o[0], NX) + ring(o[1], NY)),
)
N_PLANE = len(PLANE)
ZH_STEPS = (2, 1, 3, 0)


def two_halves(value):
    high = value.astype(BF16)
    return high, (value - high.astype(F32)).astype(BF16)


def dot(left, right):
    return lax.dot_general(left, right, (((1,), (0,)), ((), ())), preferred_element_type=F32)


def kernel(
    v_hbm, p_hbm, weight_hbm, noise_hbm, probe_hbm, spin_hbm, lace_hbm,
    out_ref,
    weight_ref, noise_ref, probe_ref, spin_ref, lace_ref,
    v_buf, p_buf, a_high, a_low, p_high, p_low, q_buf,
    s1, s1_sum, s2, y_all, w_rows, w_got,
    load_sem, small_sem, w_recv, s1_recv, s2_recv, y_recv, w_send, s1_send, s2_send, y_send,
):
    t = lax.axis_index("tm")
    s = lax.axis_index("space")
    core = lax.rem(t, NC)
    y = lax.rem(t // NC, NY)
    zl = t // (NC * NY)
    x = s // NZH
    zh = lax.rem(s, NZH)

    def device(x_, y_, zh_, zl_, c_):
        return ((zl_ * NY + y_) * NC + c_, x_ * NZH + zh_)

    small = []
    for n, (hbm, ref) in enumerate(
        (
            (weight_hbm, weight_ref),
            (noise_hbm.at[0], noise_ref),
            (probe_hbm.at[0], probe_ref),
            (spin_hbm, spin_ref),
            (lace_hbm, lace_ref),
        )
    ):
        small.append(pltpu.make_async_copy(hbm, ref, small_sem.at[n]))
    load_v = pltpu.make_async_copy(v_hbm.at[0], v_buf, load_sem.at[0])
    load_v.start()
    load_p = []
    for chunk in range(2):
        for i, zlp in enumerate(CHUNK_ZL[chunk]):
            load = pltpu.make_async_copy(
                p_hbm.at[0, :, :, pl.ds(zlp * HALF, HALF)],
                p_buf.at[:, :, pl.ds((chunk * 2 + i) * HALF, HALF)],
                load_sem.at[1 + chunk * 2 + i],
            )
            load.start()
            load_p.append(load)
    for load in small:
        load.start()

    barrier = pltpu.get_barrier_semaphore()
    for dx, dy, dc in PLANE:
        peer = device(lax.rem(x + dx, NX), lax.rem(y + dy, NY), zh, zl, lax.rem(core + dc, NC))
        pl.semaphore_signal(barrier, inc=1, device_id=peer, device_id_type=MESH)
    for dz in range(1, NZH * NZL):
        z_ = lax.rem(zh * NZL + zl + dz, NZH * NZL)
        peer = device(x, y, z_ // NZL, lax.rem(z_, NZL), core)
        pl.semaphore_signal(barrier, inc=1, device_id=peer, device_id_type=MESH)

    small[0].wait()
    n_t = NZL * NY * NC
    own = lax.broadcasted_iota(jnp.int32, (n_t, n_t), 0) == lax.broadcasted_iota(jnp.int32, (n_t, n_t), 1)
    column = jnp.sum(jnp.where(own, weight_ref[...], 0.0), axis=1, keepdims=True)
    w_rows[...] = jnp.broadcast_to(column, (n_t, HALF)).reshape(NZL, NY * NC, HALF)

    load_v.wait()
    rh, rl = two_halves(v_buf[0].T)
    ih, il = two_halves(v_buf[1].T)
    for ref, r_, i_ in ((a_high, rh, ih), (a_low, rl, il)):
        ref[:MODES, :ROWS] = r_
        ref[:MODES, ROWS:] = i_
        ref[MODES:, :ROWS] = -i_
        ref[MODES:, ROWS:] = r_

    def project(chunk):
        for i in range(2):
            load_p[chunk * 2 + i].wait()
        lanes = slice(chunk * MODES, (chunk + 1) * MODES)
        for c in range(2):
            high, low = two_halves(p_buf[c, :, lanes])
            p_high[c * ROWS : (c + 1) * ROWS, :] = high
            p_low[c * ROWS : (c + 1) * ROWS, :] = low
        ph = p_high[...]
        q = dot(a_high[...], ph) + dot(a_low[...], ph) + dot(a_high[...], p_low[...])
        for c in range(2):
            qt = q[c * MODES : (c + 1) * MODES, :].T
            for i in range(2):
                for y_ in range(NY):
                    for c_ in range(NC):
                        row = ((i * NY + y_) * NC + c_) * BLOCK
                        for h in range(2):
                            q_buf[chunk, c * 2 + h, y_, c_, i] = qt[row : row + BLOCK, h * HALF : (h + 1) * HALF]

    def scatter(chunk):
        for n, (dx, dy, dc) in enumerate(PLANE):
            x_, y_, c_ = lax.rem(x + dx, NX), lax.rem(y + dy, NY), lax.rem(core + dc, NC)
            pltpu.make_async_remote_copy(
                src_ref=q_buf.at[chunk, x_, y_, c_],
                dst_ref=s1.at[chunk, n],
                send_sem=s1_send,
                recv_sem=s1_recv.at[chunk],
                device_id=device(x_, y_, zh, zl, c_),
                device_id_type=MESH,
            ).start()

    project(0)
    pl.semaphore_wait(barrier, N_PLANE + NZH * NZL - 1)
    for n, dz in enumerate((1, NZH * NZL - 1, 2)):
        z_ = lax.rem(zh * NZL + zl + dz, NZH * NZL)
        zl_ = lax.rem(z_, NZL)
        pltpu.make_async_remote_copy(
            src_ref=w_rows.at[zl_],
            dst_ref=w_got.at[zl],
            send_sem=w_send,
            recv_sem=w_recv,
            device_id=device(x, y, z_ // NZL, zl_, core),
            device_id_type=MESH,
        ).start()
    scatter(0)
    project(1)
    scatter(1)

    w_got[zl] = w_rows[zl]

    for load in small[1:]:
        load.wait()
    er, ei = noise_ref[0], noise_ref[1]
    qr, qi = probe_ref[0], probe_ref[1]
    prod_real = er * qr + ei * qi
    prod_imag = er * qi - ei * qr
    lace_of = lax.rem(lax.broadcasted_iota(jnp.int32, (4, MODES), 1), LACE_CLASSES)
    spin_of = lax.broadcasted_iota(jnp.int32, (4, 1), 0)
    row = lax.broadcasted_iota(jnp.int32, (16, 16), 0)
    col = lax.broadcasted_iota(jnp.int32, (16, 16), 1)
    m_real = jnp.zeros((16, 16), F32)
    m_imag = jnp.zeros((16, 16), F32)
    for k in range(4):
        lace = (lace_of == lace_ref[0, k]).astype(F32)
        spin = (spin_of == spin_ref[0, k]).astype(F32)
        wr = jnp.sum(prod_real * lace, axis=1, keepdims=True) * spin
        wi = jnp.sum(prod_imag * lace, axis=1, keepdims=True) * spin
        here = (lax.div(col, 4) == k) & (lax.rem(col, 4) == lax.div(row, 4))
        m_real += jnp.where(here, jnp.concatenate([wr] * 4, axis=0), 0.0)
        m_imag += jnp.where(here, jnp.concatenate([wi] * 4, axis=0), 0.0)
    mix = jnp.concatenate(
        [jnp.concatenate([m_real, -m_imag], axis=1), jnp.concatenate([m_imag, m_real], axis=1)], axis=0
    )

    pltpu.make_async_copy(w_got.at[pl.ds(0, 3)], w_got.at[pl.ds(0, 3)], w_recv).wait()
    for chunk in range(2):
        pltpu.make_async_copy(s1.at[chunk], s1.at[chunk], s1_recv.at[chunk]).wait()
        for i, zlp in enumerate(CHUNK_ZL[chunk]):
            total = None
            for dy in range(NY):
                for dc in range(NC):
                    part = None
                    for dx in range(NX):
                        if (dx, dy, dc) == (0, 0, 0):
                            term = q_buf[chunk, x, y, core, i]
                        else:
                            term = s1[chunk, PLANE.index((dx, dy, dc)), i]
                        part = term if part is None else part + term
                    source = lax.rem(y + NY - dy, NY) * NC + lax.rem(core + dc, NC)
                    part = part * w_got[zlp, pl.ds(source, 1), :]
                    total = part if total is None else total + part
            s1_sum[chunk * 2 + i] = total
            for dzh in ZH_STEPS:
                zh_ = lax.rem(zh + dzh, NZH)

                def send(zh_=zh_, dzh=dzh, zlp=zlp, at=chunk * 2 + i):
                    pltpu.make_async_remote_copy(
                        src_ref=s1_sum.at[at],
                        dst_ref=s2.at[dzh * NZL + zl],
                        send_sem=s2_send,
                        recv_sem=s2_recv,
                        device_id=device(x, y, zh_, zlp, core),
                        device_id_type=MESH,
                    ).start()

                if dzh:
                    send()
                else:
                    pl.when(zl != zlp)(send)

                    @pl.when(zl == zlp)
                    def _(at=chunk * 2 + i):
                        s2[zl] = s1_sum[at]

    n_z = NZH * NZL - 1
    pltpu.make_async_copy(s2.at[pl.ds(0, n_z)], s2.at[pl.ds(0, n_z)], s2_recv).wait()
    total = s2[0]
    for n in range(1, n_z + 1):
        total = total + s2[n]
    y_all[x] = total
    for dx in (2, 1, 3):
        pltpu.make_async_remote_copy(
            src_ref=y_all.at[x],
            dst_ref=y_all.at[x],
            send_sem=y_send,
            recv_sem=y_recv,
            device_id=device(lax.rem(x + dx, NX), y, zh, zl, core),
            device_id_type=MESH,
        ).start()
    pltpu.make_async_copy(y_all.at[pl.ds(0, 3)], y_all.at[pl.ds(0, 3)], y_recv).wait()

    y_cat = jnp.concatenate(
        [
            jnp.concatenate([y_all[0], y_all[1]], axis=1),
            jnp.concatenate([y_all[2], y_all[3]], axis=1),
        ],
        axis=0,
    )
    z = lax.dot_general(
        mix, y_cat, (((1,), (0,)), ((), ())), precision=lax.Precision.HIGHEST, preferred_element_type=F32
    )
    z_high, z_low = two_halves(jnp.concatenate([z[:16], z[16:]], axis=1))
    both = dot(jnp.concatenate([z_high, z_low], axis=0), a_high[...])
    f = both[:16] + both[16:] + dot(z_high, a_low[...])
    out_ref[0, 0] = f[:, :ROWS]
    out_ref[0, 1] = f[:, ROWS:]

    pltpu.make_async_copy(w_got.at[pl.ds(0, 3)], w_got.at[pl.ds(0, 3)], w_send).wait()
    pltpu.make_async_copy(s1, s1, s1_send).wait()
    pltpu.make_async_copy(s2.at[pl.ds(0, n_z)], s2.at[pl.ds(0, n_z)], s2_send).wait()
    pltpu.make_async_copy(y_all.at[pl.ds(0, 3)], y_all.at[pl.ds(0, 3)], y_send).wait()


def per_device(evecs, solutions, weights, noise, probe, spin, lace):
    vmem = pl.BlockSpec(memory_space=pltpu.VMEM)
    hbm = pl.BlockSpec(memory_space=pltpu.HBM)
    dma = pltpu.SemaphoreType.DMA
    return pl.pallas_call(
        kernel,
        out_shape=jax.ShapeDtypeStruct((1, 2, BLOCK, ROWS), F32),
        in_specs=[hbm] * 7,
        out_specs=vmem,
        scratch_shapes=[
            pltpu.VMEM((1, NZL * NY * NC), F32),
            pltpu.VMEM((2, 4, MODES), F32),
            pltpu.VMEM((2, 4, MODES), F32),
            pltpu.SMEM((1, 4), jnp.int32),
            pltpu.SMEM((1, 4), jnp.int32),
            pltpu.VMEM((2, ROWS, MODES), F32),
            pltpu.VMEM((2, ROWS, 2 * MODES), F32),
            pltpu.VMEM((2 * MODES, 2 * ROWS), BF16),
            pltpu.VMEM((2 * MODES, 2 * ROWS), BF16),
            pltpu.VMEM((2 * ROWS, MODES), BF16),
            pltpu.VMEM((2 * ROWS, MODES), BF16),
            pltpu.VMEM((2, NX, NY, NC, 2, BLOCK, HALF), F32),
            pltpu.VMEM((2, N_PLANE, 2, BLOCK, HALF), F32),
            pltpu.VMEM((4, BLOCK, HALF), F32),
            pltpu.VMEM((NZH * NZL, BLOCK, HALF), F32),
            pltpu.VMEM((4, BLOCK, HALF), F32),
            pltpu.VMEM((NZL, NY * NC, HALF), F32),
            pltpu.VMEM((NZL, NY * NC, HALF), F32),
            dma((5,)), dma((5,)), dma, dma((2,)), dma, dma, dma, dma, dma, dma,
        ],
        compiler_params=pltpu.CompilerParams(
            collective_id=0, has_side_effects=True, vmem_limit_bytes=62 * 2**20
        ),
        cost_estimate=pl.CostEstimate(flops=2_500_000_000, bytes_accessed=4_900_000, transcendentals=0),
    )(evecs, solutions, weights.T, noise, probe, spin, lace)


def solution(mesh):
    placed = (
        P("tm", None, "space", None),
        P("tm", None, "space", None),
        P(None, "tm"),
        P("tm", None, None, None),
        P("tm", None, None, None),
        P("tm", None),
        P("tm", None),
    )
    return jax.shard_map(
        per_device,
        mesh=mesh,
        in_specs=placed,
        out_specs=P("tm", None, None, "space"),
        check_vma=False,
    )
```

```python
import jax
import jax.numpy as jnp
from jax import lax
from jax.experimental import pallas as pl
from jax.experimental.pallas import tpu as pltpu
from jax.sharding import PartitionSpec as P

F32 = jnp.float32
BF16 = jnp.bfloat16
MESH = pl.DeviceIdType.MESH

NX, NY, NC, NZH, NZL = 4, 4, 2, 4, 4
MODES = 256
HALF = 128
ROWS = 768
BLOCK = 16
LACE_CLASSES = 8


def ring(d, n):
    return min(d, n - d)


CHUNK_ZL = ((0, 1), (2, 3))
X_PEERS = sorted(range(1, NX), key=lambda d: -ring(d, NX))
YC_PEERS = sorted(
    [(dy, dc) for dy in range(NY) for dc in range(NC) if (dy, dc) != (0, 0)], key=lambda o: -ring(o[0], NY)
)
N_Z = NZH * NZL
FIRST_ZH, LAST_ZH = (0, 1), (2, 3)


def two_halves(value):
    high = value.astype(BF16)
    return high, (value - high.astype(F32)).astype(BF16)


def dot(left, right):
    return lax.dot_general(left, right, (((1,), (0,)), ((), ())), preferred_element_type=F32)


def kernel(
    v_hbm, p_hbm, weight_hbm, noise_hbm, probe_hbm, spin_hbm, lace_hbm,
    out_ref,
    weight_ref, noise_ref, probe_ref, spin_ref, lace_ref,
    v_buf, p_buf, v_t, p_high, p_low, qx_buf, qy_buf,
    x1, y1, x_sum, y_sum, y2, x2, s1_sum, s2, y_all, w_rows, w_got,
    load_sem, small_sem, w_recv, x1_recv, y1_recv, y2_recv, x2_recv, s2_recv, y_recv, send_sem, near_sem, far_sem,
):
    t = lax.axis_index("tm")
    s = lax.axis_index("space")
    core = lax.rem(t, NC)
    y = lax.rem(t // NC, NY)
    zl = t // (NC * NY)
    x = s // NZH
    zh = lax.rem(s, NZH)

    def device(x_, y_, zh_, zl_, c_):
        return ((zl_ * NY + y_) * NC + c_, x_ * NZH + zh_)

    z = zh * NZL + zl

    def z_peer(dz):
        z_ = z + dz
        return device(x, y, z_ // NZL, lax.rem(z_, NZL), core)

    def x_peer(dx):
        return device(lax.rem(x + dx, NX), y, zh, zl, core)

    def yc_peer(dy, dc):
        return device(x, lax.rem(y + dy, NY), zh, zl, lax.rem(core + dc, NC))

    small = []
    for n, (hbm, ref) in enumerate(
        (
            (weight_hbm, weight_ref),
            (noise_hbm.at[0], noise_ref),
            (probe_hbm.at[0], probe_ref),
            (spin_hbm, spin_ref),
            (lace_hbm, lace_ref),
        )
    ):
        small.append(pltpu.make_async_copy(hbm, ref, small_sem.at[n]))
    load_v = [pltpu.make_async_copy(v_hbm.at[0, c], v_buf.at[c], load_sem.at[c]) for c in range(2)]
    load_p = [
        pltpu.make_async_copy(
            p_hbm.at[0, :, :, pl.ds(chunk * MODES, MODES)],
            p_buf.at[:, :, pl.ds(chunk * MODES, MODES)],
            load_sem.at[2 + chunk],
        )
        for chunk in range(2)
    ]
    for load in load_v + load_p:
        load.start()
    for load in small:
        load.start()

    def keep_v(n, value):
        rows = slice(n * ROWS, (n + 1) * ROWS)
        v_t[:MODES, rows], v_t[MODES:, rows] = two_halves(value)

    barrier = pltpu.get_barrier_semaphore()
    for dx in X_PEERS:
        pl.semaphore_signal(barrier, inc=1, device_id=x_peer(dx), device_id_type=MESH)
    for dy, dc in YC_PEERS:
        pl.semaphore_signal(barrier, inc=1, device_id=yc_peer(dy, dc), device_id_type=MESH)
    for dz in range(1, N_Z):

        @pl.when(z + dz < N_Z)
        def _():
            pl.semaphore_signal(barrier, inc=1, device_id=z_peer(dz), device_id_type=MESH)

    small[0].wait()
    n_t = NZL * NY * NC
    own = lax.broadcasted_iota(jnp.int32, (n_t, n_t), 0) == lax.broadcasted_iota(jnp.int32, (n_t, n_t), 1)
    column = jnp.sum(jnp.where(own, weight_ref[...], 0.0), axis=1, keepdims=True)
    w_rows[...] = jnp.broadcast_to(column, (n_t, HALF)).reshape(NZL, NY * NC, HALF)

    load_v[0].wait()
    v_real = v_buf[0].T
    keep_v(0, v_real)
    load_v[1].wait()
    v_imag = v_buf[1].T
    keep_v(1, v_imag)
    keep_v(2, v_real - v_imag)

    def product(n, value):
        rows = slice(n * ROWS, (n + 1) * ROWS)
        p_high[rows, :], p_low[rows, :] = two_halves(value)
        both = dot(v_t[:, rows], p_high[rows, :])
        return both[:MODES] + both[MODES:] + dot(v_t[:MODES, rows], p_low[rows, :])

    def keep_q(chunk, c, q):
        qt = q.T
        for y_ in range(NY):
            for c_ in range(NC):
                for h in range(2):
                    lanes = slice(h * HALF, (h + 1) * HALF)
                    row = (y_ * NC + c_) * BLOCK
                    qx_buf[chunk, c * 2 + h, y_ * NC + c_] = qt[row : row + BLOCK, lanes]
                    row += HALF
                    qy_buf[chunk, y_ * NC + c_, c * 2 + h] = qt[row : row + BLOCK, lanes]

    def project(chunk):
        load_p[chunk].wait()
        lanes = slice(chunk * MODES, (chunk + 1) * MODES)
        p_real, p_imag = p_buf[0, :, lanes], p_buf[1, :, lanes]
        rr = product(0, p_real)
        ii = product(1, p_imag)
        keep_q(chunk, 0, rr + ii)
        keep_q(chunk, 1, product(2, p_real + p_imag) - rr + ii)

    def send(src, dst, send_sem, recv_sem, to):
        pltpu.make_async_remote_copy(
            src_ref=src, dst_ref=dst, send_sem=send_sem, recv_sem=recv_sem, device_id=to, device_id_type=MESH
        ).start()

    def yc_index(dy, dc):
        return lax.rem(y + dy, NY) * NC + lax.rem(core + dc, NC)

    def arrived(ref, sem):
        pltpu.make_async_copy(ref, ref, sem).wait()

    def scatter(chunk):
        for n in range(len(YC_PEERS)):
            dy, dc = YC_PEERS[n]
            send(qy_buf.at[chunk, yc_index(dy, dc)], y1.at[chunk, n], send_sem.at[1], y1_recv.at[chunk], yc_peer(dy, dc))
            if n < len(X_PEERS):
                dx = X_PEERS[n]
                send(qx_buf.at[chunk, lax.rem(x + dx, NX)], x1.at[chunk, n], send_sem.at[0], x1_recv.at[chunk], x_peer(dx))

    def weighted(zlp, own, others):
        total = own * w_got[zlp, pl.ds(y * NC + core, 1), :]
        for n, (dy, dc) in enumerate(YC_PEERS):
            source = lax.rem(y + NY - dy, NY) * NC + lax.rem(core + dc, NC)
            total = total + others[n] * w_got[zlp, pl.ds(source, 1), :]
        return total

    def across(chunk):
        arrived(x1.at[chunk], x1_recv.at[chunk])
        total = qx_buf[chunk, x]
        for n in range(len(X_PEERS)):
            total = total + x1[chunk, n]
        x_sum[chunk] = total
        for n, (dy, dc) in enumerate(YC_PEERS):
            send(x_sum.at[chunk, yc_index(dy, dc)], y2.at[chunk, n], send_sem.at[2], y2_recv.at[chunk], yc_peer(dy, dc))
        arrived(y1.at[chunk], y1_recv.at[chunk])
        zlp = CHUNK_ZL[chunk][1]
        for x_ in range(NX):
            y_sum[chunk, x_] = weighted(
                zlp, qy_buf[chunk, y * NC + core, x_], [y1[chunk, n, x_] for n in range(len(YC_PEERS))]
            )
        for n, dx in enumerate(X_PEERS):
            send(y_sum.at[chunk, lax.rem(x + dx, NX)], x2.at[chunk, n], send_sem.at[3], x2_recv.at[chunk], x_peer(dx))

    def along_z(chunk, i):
        zlp, at = CHUNK_ZL[chunk][i], chunk * 2 + i
        if i == 0:
            arrived(y2.at[chunk], y2_recv.at[chunk])
            total = weighted(zlp, x_sum[chunk, y * NC + core], [y2[chunk, n] for n in range(len(YC_PEERS))])
        else:
            arrived(x2.at[chunk], x2_recv.at[chunk])
            total = y_sum[chunk, x]
            for n in range(len(X_PEERS)):
                total = total + x2[chunk, n]
        s1_sum[at] = total

    def to_z(at, zh_):
        zlp = CHUNK_ZL[at // 2][at % 2]
        here = z == zh_ * NZL + zlp

        @pl.when(jnp.logical_not(here))
        def _():
            send(s1_sum.at[at], s2.at[z], send_sem.at[4], s2_recv, device(x, y, zh_, zlp, core))

        @pl.when(here)
        def _():
            s2[z] = s1_sum[at]

    project(0)
    pl.semaphore_wait(barrier, len(X_PEERS) + len(YC_PEERS) + z)
    for dz in range(1, NZL):

        @pl.when(dz <= zl)
        def _():
            pl.semaphore_signal(near_sem, inc=1, device_id=z_peer(-dz), device_id_type=MESH)
            send(w_rows.at[zl - dz], w_got.at[zl], send_sem.at[5], w_recv, z_peer(-dz))

    scatter(0)
    project(1)
    scatter(1)

    for dz in range(1, N_Z):

        @pl.when((dz > zl) & (dz <= z))
        def _():
            pl.semaphore_signal(far_sem, inc=1, device_id=z_peer(-dz), device_id_type=MESH)

    w_got[zl] = w_rows[zl]

    @pl.when(zl < NZL - 1)
    def _():
        pl.semaphore_wait(near_sem, NZL - 1 - zl)

    for dz in range(1, NZL):

        @pl.when(zl + dz < NZL)
        def _():
            send(w_rows.at[zl + dz], w_got.at[zl], send_sem.at[5], w_recv, z_peer(dz))


    for load in small[1:]:
        load.wait()
    er, ei = noise_ref[0], noise_ref[1]
    qr, qi = probe_ref[0], probe_ref[1]
    prod_real = er * qr + ei * qi
    prod_imag = er * qi - ei * qr
    lace_of = lax.rem(lax.broadcasted_iota(jnp.int32, (4, MODES), 1), LACE_CLASSES)
    spin_of = lax.broadcasted_iota(jnp.int32, (4, 1), 0)
    row = lax.broadcasted_iota(jnp.int32, (16, 16), 0)
    col = lax.broadcasted_iota(jnp.int32, (16, 16), 1)
    m_real = jnp.zeros((16, 16), F32)
    m_imag = jnp.zeros((16, 16), F32)
    for k in range(4):
        lace = (lace_of == lace_ref[0, k]).astype(F32)
        spin = (spin_of == spin_ref[0, k]).astype(F32)
        wr = jnp.sum(prod_real * lace, axis=1, keepdims=True) * spin
        wi = jnp.sum(prod_imag * lace, axis=1, keepdims=True) * spin
        here = (lax.div(col, 4) == k) & (lax.rem(col, 4) == lax.div(row, 4))
        m_real += jnp.where(here, jnp.concatenate([wr] * 4, axis=0), 0.0)
        m_imag += jnp.where(here, jnp.concatenate([wi] * 4, axis=0), 0.0)
    mix = jnp.concatenate(
        [jnp.concatenate([m_real, -m_imag], axis=1), jnp.concatenate([m_imag, m_real], axis=1)], axis=0
    )

    arrived(w_got.at[pl.ds(0, 3)], w_recv)
    across(0)
    across(1)

    @pl.when(zh < NZH - 1)
    def _():
        pl.semaphore_wait(far_sem, (NZH - 1 - zh) * NZL)

    for chunk in range(2):
        for i in range(2):
            along_z(chunk, i)
            for zh_ in FIRST_ZH:
                to_z(chunk * 2 + i, zh_)
    for at in range(4):
        for zh_ in LAST_ZH:
            to_z(at, zh_)

    n_z = NZH * NZL - 1
    arrived(s2.at[pl.ds(0, n_z)], s2_recv)
    total = s2[0]
    for n in range(1, n_z + 1):
        total = total + s2[n]
    y_all[x] = total
    for dx in X_PEERS:
        send(y_all.at[x], y_all.at[x], send_sem.at[6], y_recv, x_peer(dx))
    arrived(y_all.at[pl.ds(0, 3)], y_recv)

    y_cat = jnp.concatenate(
        [
            jnp.concatenate([y_all[0], y_all[1]], axis=1),
            jnp.concatenate([y_all[2], y_all[3]], axis=1),
        ],
        axis=0,
    )
    z_cat = lax.dot_general(
        mix, y_cat, (((1,), (0,)), ((), ())), precision=lax.Precision.HIGHEST, preferred_element_type=F32
    )
    z_high, z_low = two_halves(z_cat)
    z_both = jnp.concatenate([z_high, z_low], axis=0)
    f = []
    for n in range(2):
        rows = slice(n * ROWS, (n + 1) * ROWS)
        both = dot(z_both, v_t[:MODES, rows])
        f.append(both[:32] + both[32:] + dot(z_high, v_t[MODES:, rows]))
    out_ref[0, 0] = f[0][:16] - f[1][16:]
    out_ref[0, 1] = f[0][16:] + f[1][:16]

    for n, ref in enumerate(
        (x1, y1, y2, x2, s2.at[pl.ds(0, n_z)], w_got.at[pl.ds(0, 3)], y_all.at[pl.ds(0, 3)])
    ):
        arrived(ref, send_sem.at[n])


def per_device(evecs, solutions, weights, noise, probe, spin, lace):
    vmem = pl.BlockSpec(memory_space=pltpu.VMEM)
    hbm = pl.BlockSpec(memory_space=pltpu.HBM)
    dma = pltpu.SemaphoreType.DMA
    return pl.pallas_call(
        kernel,
        out_shape=jax.ShapeDtypeStruct((1, 2, BLOCK, ROWS), F32),
        in_specs=[hbm] * 7,
        out_specs=vmem,
        scratch_shapes=[
            pltpu.VMEM((1, NZL * NY * NC), F32),
            pltpu.VMEM((2, 4, MODES), F32),
            pltpu.VMEM((2, 4, MODES), F32),
            pltpu.SMEM((1, 4), jnp.int32),
            pltpu.SMEM((1, 4), jnp.int32),
            pltpu.VMEM((2, ROWS, MODES), F32),
            pltpu.VMEM((2, ROWS, 2 * MODES), F32),
            pltpu.VMEM((2 * MODES, 3 * ROWS), BF16),
            pltpu.VMEM((3 * ROWS, MODES), BF16),
            pltpu.VMEM((3 * ROWS, MODES), BF16),
            pltpu.VMEM((2, NX, NY * NC, BLOCK, HALF), F32),
            pltpu.VMEM((2, NY * NC, NX, BLOCK, HALF), F32),
            pltpu.VMEM((2, len(X_PEERS), NY * NC, BLOCK, HALF), F32),
            pltpu.VMEM((2, len(YC_PEERS), NX, BLOCK, HALF), F32),
            pltpu.VMEM((2, NY * NC, BLOCK, HALF), F32),
            pltpu.VMEM((2, NX, BLOCK, HALF), F32),
            pltpu.VMEM((2, len(YC_PEERS), BLOCK, HALF), F32),
            pltpu.VMEM((2, len(X_PEERS), BLOCK, HALF), F32),
            pltpu.VMEM((4, BLOCK, HALF), F32),
            pltpu.VMEM((NZH * NZL, BLOCK, HALF), F32),
            pltpu.VMEM((4, BLOCK, HALF), F32),
            pltpu.VMEM((NZL, NY * NC, HALF), F32),
            pltpu.VMEM((NZL, NY * NC, HALF), F32),
            dma((4,)), dma((5,)), dma, dma((2,)), dma((2,)), dma((2,)), dma((2,)), dma, dma, dma((7,)),
            pltpu.SemaphoreType.REGULAR, pltpu.SemaphoreType.REGULAR,
        ],
        compiler_params=pltpu.CompilerParams(
            collective_id=0, has_side_effects=True, vmem_limit_bytes=62 * 2**20
        ),
        cost_estimate=pl.CostEstimate(flops=2_500_000_000, bytes_accessed=4_900_000, transcendentals=0),
    )(evecs, solutions, weights.T, noise, probe, spin, lace)


def solution(mesh):
    placed = (
        P("tm", None, "space", None),
        P("tm", None, "space", None),
        P(None, "tm"),
        P("tm", None, None, None),
        P("tm", None, None, None),
        P("tm", None),
        P("tm", None),
    )
    return jax.shard_map(
        per_device,
        mesh=mesh,
        in_specs=placed,
        out_specs=P("tm", None, None, "space"),
        check_vma=False,
    )
```

```python
import jax
import jax.numpy as jnp
from jax import lax
from jax.experimental import pallas as pl
from jax.experimental.pallas import tpu as pltpu
from jax.sharding import PartitionSpec as P

F32 = jnp.float32
BF16 = jnp.bfloat16
MESH = pl.DeviceIdType.MESH

NX, NY, NC, NZH, NZL = 4, 4, 2, 4, 4
MODES = 256
HALF = 128
ROWS = 768
BLOCK = 16
LACE_CLASSES = 8


def ring(d, n):
    return min(d, n - d)


CHUNK_ZL = ((0, 1), (2, 3))
X_PEERS = sorted(range(1, NX), key=lambda d: -ring(d, NX))
YC_PEERS = sorted(
    [(dy, dc) for dy in range(NY) for dc in range(NC) if (dy, dc) != (0, 0)], key=lambda o: -ring(o[0], NY)
)
N_Z = NZH * NZL
FIRST_ZH, LAST_ZH = (0, 1), (2, 3)


def two_halves(value):
    high = value.astype(BF16)
    return high, (value - high.astype(F32)).astype(BF16)


def dot(left, right):
    return lax.dot_general(left, right, (((1,), (0,)), ((), ())), preferred_element_type=F32)


def kernel(
    v_hbm, p_hbm, weight_hbm, noise_hbm, probe_hbm, spin_hbm, lace_hbm,
    out_ref,
    weight_ref, noise_ref, probe_ref, spin_ref, lace_ref,
    v_buf, p_buf, v_t, p_high, p_low, qx_buf, qy_buf,
    x1, y1, x_sum, y_sum, y2, x2, s1_sum, s2, y_all, w_rows, w_got,
    load_sem, small_sem, w_recv, x1_recv, y1_recv, y2_recv, x2_recv, s2_recv, y_recv, send_sem, near_sem, far_sem,
):
    t = lax.axis_index("tm")
    s = lax.axis_index("space")
    core = lax.rem(t, NC)
    y = lax.rem(t // NC, NY)
    zl = t // (NC * NY)
    x = s // NZH
    zh = lax.rem(s, NZH)

    def device(x_, y_, zh_, zl_, c_):
        return ((zl_ * NY + y_) * NC + c_, x_ * NZH + zh_)

    z = zh * NZL + zl

    def z_peer(dz):
        z_ = z + dz
        return device(x, y, z_ // NZL, lax.rem(z_, NZL), core)

    def x_peer(dx):
        return device(lax.rem(x + dx, NX), y, zh, zl, core)

    def yc_peer(dy, dc):
        return device(x, lax.rem(y + dy, NY), zh, zl, lax.rem(core + dc, NC))

    small = []
    for n, (hbm, ref) in enumerate(
        (
            (weight_hbm, weight_ref),
            (noise_hbm.at[0], noise_ref),
            (probe_hbm.at[0], probe_ref),
            (spin_hbm, spin_ref),
            (lace_hbm, lace_ref),
        )
    ):
        small.append(pltpu.make_async_copy(hbm, ref, small_sem.at[n]))
    load_v = [pltpu.make_async_copy(v_hbm.at[0, c], v_buf.at[c], load_sem.at[c]) for c in range(2)]
    load_p = [
        [
            pltpu.make_async_copy(
                p_hbm.at[0, c, :, pl.ds(chunk * MODES, MODES)],
                p_buf.at[c, :, pl.ds(chunk * MODES, MODES)],
                load_sem.at[2 + chunk * 2 + c],
            )
            for c in range(2)
        ]
        for chunk in range(2)
    ]
    for c in range(2):
        load_v[c].start()
        load_p[0][c].start()
    for c in range(2):
        load_p[1][c].start()
    for load in small:
        load.start()

    def keep_v(n, value):
        rows = slice(n * ROWS, (n + 1) * ROWS)
        v_t[:MODES, rows], v_t[MODES:, rows] = two_halves(value)

    barrier = pltpu.get_barrier_semaphore()
    for dx in X_PEERS:
        pl.semaphore_signal(barrier, inc=1, device_id=x_peer(dx), device_id_type=MESH)
    for dy, dc in YC_PEERS:
        pl.semaphore_signal(barrier, inc=1, device_id=yc_peer(dy, dc), device_id_type=MESH)
    for dz in range(1, N_Z):

        @pl.when(z + dz < N_Z)
        def _():
            pl.semaphore_signal(barrier, inc=1, device_id=z_peer(dz), device_id_type=MESH)

    small[0].wait()
    n_t = NZL * NY * NC
    own = lax.broadcasted_iota(jnp.int32, (n_t, n_t), 0) == lax.broadcasted_iota(jnp.int32, (n_t, n_t), 1)
    column = jnp.sum(jnp.where(own, weight_ref[...], 0.0), axis=1, keepdims=True)
    w_rows[...] = jnp.broadcast_to(column, (n_t, HALF)).reshape(NZL, NY * NC, HALF)

    def product(n, value):
        rows = slice(n * ROWS, (n + 1) * ROWS)
        p_high[rows, :], p_low[rows, :] = two_halves(value)
        both = dot(v_t[:, rows], p_high[rows, :])
        return both[:MODES] + both[MODES:] + dot(v_t[:MODES, rows], p_low[rows, :])

    def keep_q(chunk, c, q):
        qt = q.T
        for y_ in range(NY):
            for c_ in range(NC):
                for h in range(2):
                    lanes = slice(h * HALF, (h + 1) * HALF)
                    row = (y_ * NC + c_) * BLOCK
                    qx_buf[chunk, c * 2 + h, y_ * NC + c_] = qt[row : row + BLOCK, lanes]
                    row += HALF
                    qy_buf[chunk, y_ * NC + c_, c * 2 + h] = qt[row : row + BLOCK, lanes]

    def project(chunk):
        lanes = slice(chunk * MODES, (chunk + 1) * MODES)
        if chunk == 0:
            load_v[0].wait()
            v_real = v_buf[0].T
            keep_v(0, v_real)
        load_p[chunk][0].wait()
        rr = product(0, p_buf[0, :, lanes])
        if chunk == 0:
            load_v[1].wait()
            v_imag = v_buf[1].T
            keep_v(1, v_imag)
            keep_v(2, v_real - v_imag)
        load_p[chunk][1].wait()
        ii = product(1, p_buf[1, :, lanes])
        keep_q(chunk, 0, rr + ii)
        keep_q(chunk, 1, product(2, p_buf[0, :, lanes] + p_buf[1, :, lanes]) - rr + ii)

    def send(src, dst, send_sem, recv_sem, to):
        pltpu.make_async_remote_copy(
            src_ref=src, dst_ref=dst, send_sem=send_sem, recv_sem=recv_sem, device_id=to, device_id_type=MESH
        ).start()

    def yc_index(dy, dc):
        return lax.rem(y + dy, NY) * NC + lax.rem(core + dc, NC)

    def arrived(ref, sem):
        pltpu.make_async_copy(ref, ref, sem).wait()

    def scatter(chunk):
        for n in range(len(YC_PEERS)):
            dy, dc = YC_PEERS[n]
            send(qy_buf.at[chunk, yc_index(dy, dc)], y1.at[chunk, n], send_sem.at[1], y1_recv.at[chunk], yc_peer(dy, dc))
            if n < len(X_PEERS):
                dx = X_PEERS[n]
                send(qx_buf.at[chunk, lax.rem(x + dx, NX)], x1.at[chunk, n], send_sem.at[0], x1_recv.at[chunk], x_peer(dx))

    def weighted(zlp, own, others):
        total = own * w_got[zlp, pl.ds(y * NC + core, 1), :]
        for n, (dy, dc) in enumerate(YC_PEERS):
            source = lax.rem(y + NY - dy, NY) * NC + lax.rem(core + dc, NC)
            total = total + others[n] * w_got[zlp, pl.ds(source, 1), :]
        return total

    def across(chunk):
        arrived(x1.at[chunk], x1_recv.at[chunk])
        total = qx_buf[chunk, x]
        for n in range(len(X_PEERS)):
            total = total + x1[chunk, n]
        x_sum[chunk] = total
        for n, (dy, dc) in enumerate(YC_PEERS):
            send(x_sum.at[chunk, yc_index(dy, dc)], y2.at[chunk, n], send_sem.at[2], y2_recv.at[chunk], yc_peer(dy, dc))
        arrived(y1.at[chunk], y1_recv.at[chunk])
        zlp = CHUNK_ZL[chunk][1]
        for x_ in range(NX):
            y_sum[chunk, x_] = weighted(
                zlp, qy_buf[chunk, y * NC + core, x_], [y1[chunk, n, x_] for n in range(len(YC_PEERS))]
            )
        for n, dx in enumerate(X_PEERS):
            send(y_sum.at[chunk, lax.rem(x + dx, NX)], x2.at[chunk, n], send_sem.at[3], x2_recv.at[chunk], x_peer(dx))

    def along_z(chunk, i):
        zlp, at = CHUNK_ZL[chunk][i], chunk * 2 + i
        if i == 0:
            arrived(y2.at[chunk], y2_recv.at[chunk])
            total = weighted(zlp, x_sum[chunk, y * NC + core], [y2[chunk, n] for n in range(len(YC_PEERS))])
        else:
            arrived(x2.at[chunk], x2_recv.at[chunk])
            total = y_sum[chunk, x]
            for n in range(len(X_PEERS)):
                total = total + x2[chunk, n]
        s1_sum[at] = total

    def to_z(at, zh_):
        zlp = CHUNK_ZL[at // 2][at % 2]
        here = z == zh_ * NZL + zlp

        @pl.when(jnp.logical_not(here))
        def _():
            send(s1_sum.at[at], s2.at[z], send_sem.at[4], s2_recv, device(x, y, zh_, zlp, core))

        @pl.when(here)
        def _():
            s2[z] = s1_sum[at]

    project(0)
    pl.semaphore_wait(barrier, len(X_PEERS) + len(YC_PEERS) + z)
    for dz in range(1, NZL):

        @pl.when(dz <= zl)
        def _():
            pl.semaphore_signal(near_sem, inc=1, device_id=z_peer(-dz), device_id_type=MESH)
            send(w_rows.at[zl - dz], w_got.at[zl], send_sem.at[5], w_recv, z_peer(-dz))

    scatter(0)
    project(1)
    scatter(1)

    for dz in range(1, N_Z):

        @pl.when((dz > zl) & (dz <= z))
        def _():
            pl.semaphore_signal(far_sem, inc=1, device_id=z_peer(-dz), device_id_type=MESH)

    w_got[zl] = w_rows[zl]

    @pl.when(zl < NZL - 1)
    def _():
        pl.semaphore_wait(near_sem, NZL - 1 - zl)

    for dz in range(1, NZL):

        @pl.when(zl + dz < NZL)
        def _():
            send(w_rows.at[zl + dz], w_got.at[zl], send_sem.at[5], w_recv, z_peer(dz))


    for load in small[1:]:
        load.wait()
    er, ei = noise_ref[0], noise_ref[1]
    qr, qi = probe_ref[0], probe_ref[1]
    prod_real = er * qr + ei * qi
    prod_imag = er * qi - ei * qr
    lace_of = lax.rem(lax.broadcasted_iota(jnp.int32, (4, MODES), 1), LACE_CLASSES)
    spin_of = lax.broadcasted_iota(jnp.int32, (4, 1), 0)
    row = lax.broadcasted_iota(jnp.int32, (16, 16), 0)
    col = lax.broadcasted_iota(jnp.int32, (16, 16), 1)
    m_real = jnp.zeros((16, 16), F32)
    m_imag = jnp.zeros((16, 16), F32)
    for k in range(4):
        lace = (lace_of == lace_ref[0, k]).astype(F32)
        spin = (spin_of == spin_ref[0, k]).astype(F32)
        wr = jnp.sum(prod_real * lace, axis=1, keepdims=True) * spin
        wi = jnp.sum(prod_imag * lace, axis=1, keepdims=True) * spin
        here = (lax.div(col, 4) == k) & (lax.rem(col, 4) == lax.div(row, 4))
        m_real += jnp.where(here, jnp.concatenate([wr] * 4, axis=0), 0.0)
        m_imag += jnp.where(here, jnp.concatenate([wi] * 4, axis=0), 0.0)
    mix = jnp.concatenate(
        [jnp.concatenate([m_real, -m_imag], axis=1), jnp.concatenate([m_imag, m_real], axis=1)], axis=0
    )

    arrived(w_got.at[pl.ds(0, 3)], w_recv)
    across(0)
    across(1)

    @pl.when(zh < NZH - 1)
    def _():
        pl.semaphore_wait(far_sem, (NZH - 1 - zh) * NZL)

    for chunk in range(2):
        for i in range(2):
            along_z(chunk, i)
            to_z(chunk * 2 + i, 0)
        for at in range(chunk * 2, chunk * 2 + 2):
            to_z(at, 1)
    for zh_ in range(2, NZH):
        for at in range(4):
            to_z(at, zh_)

    n_z = NZH * NZL - 1
    arrived(s2.at[pl.ds(0, n_z)], s2_recv)
    total = s2[0]
    for n in range(1, n_z + 1):
        total = total + s2[n]
    y_all[x] = total
    for dx in X_PEERS:
        send(y_all.at[x], y_all.at[x], send_sem.at[6], y_recv, x_peer(dx))
    arrived(y_all.at[pl.ds(0, 3)], y_recv)

    y_cat = jnp.concatenate(
        [
            jnp.concatenate([y_all[0], y_all[1]], axis=1),
            jnp.concatenate([y_all[2], y_all[3]], axis=1),
        ],
        axis=0,
    )
    z_cat = lax.dot_general(
        mix, y_cat, (((1,), (0,)), ((), ())), precision=lax.Precision.HIGHEST, preferred_element_type=F32
    )
    z_high, z_low = two_halves(z_cat)
    z_both = jnp.concatenate([z_high, z_low], axis=0)
    f = []
    for n in range(2):
        rows = slice(n * ROWS, (n + 1) * ROWS)
        both = dot(z_both, v_t[:MODES, rows])
        f.append(both[:32] + both[32:] + dot(z_high, v_t[MODES:, rows]))
    out_ref[0, 0] = f[0][:16] - f[1][16:]
    out_ref[0, 1] = f[0][16:] + f[1][:16]

    for n, ref in enumerate(
        (x1, y1, y2, x2, s2.at[pl.ds(0, n_z)], w_got.at[pl.ds(0, 3)], y_all.at[pl.ds(0, 3)])
    ):
        arrived(ref, send_sem.at[n])


def per_device(evecs, solutions, weights, noise, probe, spin, lace):
    vmem = pl.BlockSpec(memory_space=pltpu.VMEM)
    hbm = pl.BlockSpec(memory_space=pltpu.HBM)
    dma = pltpu.SemaphoreType.DMA
    return pl.pallas_call(
        kernel,
        out_shape=jax.ShapeDtypeStruct((1, 2, BLOCK, ROWS), F32),
        in_specs=[hbm] * 7,
        out_specs=vmem,
        scratch_shapes=[
            pltpu.VMEM((1, NZL * NY * NC), F32),
            pltpu.VMEM((2, 4, MODES), F32),
            pltpu.VMEM((2, 4, MODES), F32),
            pltpu.SMEM((1, 4), jnp.int32),
            pltpu.SMEM((1, 4), jnp.int32),
            pltpu.VMEM((2, ROWS, MODES), F32),
            pltpu.VMEM((2, ROWS, 2 * MODES), F32),
            pltpu.VMEM((2 * MODES, 3 * ROWS), BF16),
            pltpu.VMEM((3 * ROWS, MODES), BF16),
            pltpu.VMEM((3 * ROWS, MODES), BF16),
            pltpu.VMEM((2, NX, NY * NC, BLOCK, HALF), F32),
            pltpu.VMEM((2, NY * NC, NX, BLOCK, HALF), F32),
            pltpu.VMEM((2, len(X_PEERS), NY * NC, BLOCK, HALF), F32),
            pltpu.VMEM((2, len(YC_PEERS), NX, BLOCK, HALF), F32),
            pltpu.VMEM((2, NY * NC, BLOCK, HALF), F32),
            pltpu.VMEM((2, NX, BLOCK, HALF), F32),
            pltpu.VMEM((2, len(YC_PEERS), BLOCK, HALF), F32),
            pltpu.VMEM((2, len(X_PEERS), BLOCK, HALF), F32),
            pltpu.VMEM((4, BLOCK, HALF), F32),
            pltpu.VMEM((NZH * NZL, BLOCK, HALF), F32),
            pltpu.VMEM((4, BLOCK, HALF), F32),
            pltpu.VMEM((NZL, NY * NC, HALF), F32),
            pltpu.VMEM((NZL, NY * NC, HALF), F32),
            dma((6,)), dma((5,)), dma, dma((2,)), dma((2,)), dma((2,)), dma((2,)), dma, dma, dma((7,)),
            pltpu.SemaphoreType.REGULAR, pltpu.SemaphoreType.REGULAR,
        ],
        compiler_params=pltpu.CompilerParams(
            collective_id=0, has_side_effects=True, vmem_limit_bytes=62 * 2**20
        ),
        cost_estimate=pl.CostEstimate(flops=2_500_000_000, bytes_accessed=4_900_000, transcendentals=0),
    )(evecs, solutions, weights.T, noise, probe, spin, lace)


def solution(mesh):
    placed = (
        P("tm", None, "space", None),
        P("tm", None, "space", None),
        P(None, "tm"),
        P("tm", None, None, None),
        P("tm", None, None, None),
        P("tm", None),
        P("tm", None),
    )
    return jax.shard_map(
        per_device,
        mesh=mesh,
        in_specs=placed,
        out_specs=P("tm", None, None, "space"),
        check_vma=False,
    )
```

```python
import jax
import jax.numpy as jnp
from jax import lax
from jax.experimental import pallas as pl
from jax.experimental.pallas import tpu as pltpu
from jax.sharding import PartitionSpec as P

F32 = jnp.float32
BF16 = jnp.bfloat16
MESH = pl.DeviceIdType.MESH

NX, NY, NC, NZH, NZL = 4, 4, 2, 4, 4
MODES = 256
HALF = 128
ROWS = 768
BLOCK = 16
LACE_CLASSES = 8


def ring(d, n):
    return min(d, n - d)


CHUNK_ZL = ((0, 1), (2, 3))
X_PEERS = sorted(range(1, NX), key=lambda d: -ring(d, NX))
YC_PEERS = sorted(
    [(dy, dc) for dy in range(NY) for dc in range(NC) if (dy, dc) != (0, 0)], key=lambda o: -ring(o[0], NY)
)
N_Z = NZH * NZL
FIRST_ZH, LAST_ZH = (0, 1), (2, 3)


def two_halves(value):
    high = value.astype(BF16)
    return high, (value - high.astype(F32)).astype(BF16)


def dot(left, right):
    return lax.dot_general(left, right, (((1,), (0,)), ((), ())), preferred_element_type=F32)


def kernel(
    v_hbm, p_hbm, weight_hbm, noise_hbm, probe_hbm, spin_hbm, lace_hbm,
    out_ref,
    weight_ref, noise_ref, probe_ref, spin_ref, lace_ref,
    v_buf, p_buf, v_t, p_high, p_low, qx_buf, qy_buf,
    x1, y1, x_sum, y_sum, y2, x2, s1_sum, s2, y_all, w_rows, w_got,
    load_sem, small_sem, w_recv, x1_recv, y1_recv, y2_recv, x2_recv, s2_recv, y_recv, send_sem, near_sem, far_sem, out_buf, out_sem,
):
    t = lax.axis_index("tm")
    s = lax.axis_index("space")
    core = lax.rem(t, NC)
    y = lax.rem(t // NC, NY)
    zl = t // (NC * NY)
    x = s // NZH
    zh = lax.rem(s, NZH)

    def device(x_, y_, zh_, zl_, c_):
        return ((zl_ * NY + y_) * NC + c_, x_ * NZH + zh_)

    z = zh * NZL + zl

    def z_peer(dz):
        z_ = z + dz
        return device(x, y, z_ // NZL, lax.rem(z_, NZL), core)

    def x_peer(dx):
        return device(lax.rem(x + dx, NX), y, zh, zl, core)

    def yc_peer(dy, dc):
        return device(x, lax.rem(y + dy, NY), zh, zl, lax.rem(core + dc, NC))

    small = []
    for n, (hbm, ref) in enumerate(
        (
            (weight_hbm, weight_ref),
            (noise_hbm.at[0], noise_ref),
            (probe_hbm.at[0], probe_ref),
            (spin_hbm, spin_ref),
            (lace_hbm, lace_ref),
        )
    ):
        small.append(pltpu.make_async_copy(hbm, ref, small_sem.at[n]))
    load_v = [pltpu.make_async_copy(v_hbm.at[0, c], v_buf.at[c], load_sem.at[c]) for c in range(2)]
    load_p = [
        [
            pltpu.make_async_copy(
                p_hbm.at[0, c, :, pl.ds(chunk * MODES, MODES)],
                p_buf.at[c, :, pl.ds(chunk * MODES, MODES)],
                load_sem.at[2 + chunk * 2 + c],
            )
            for c in range(2)
        ]
        for chunk in range(2)
    ]
    for c in range(2):
        load_v[c].start()
        load_p[0][c].start()
    barrier = pltpu.get_barrier_semaphore()
    for dx in X_PEERS:
        pl.semaphore_signal(barrier, inc=1, device_id=x_peer(dx), device_id_type=MESH)
    for dy, dc in YC_PEERS:
        pl.semaphore_signal(barrier, inc=1, device_id=yc_peer(dy, dc), device_id_type=MESH)
    for c in range(2):
        load_p[1][c].start()
    for load in small:
        load.start()

    def keep_v(n, value):
        rows = slice(n * ROWS, (n + 1) * ROWS)
        v_t[:MODES, rows], v_t[MODES:, rows] = two_halves(value)

    for dz in range(1, N_Z):

        @pl.when(z + dz < N_Z)
        def _():
            pl.semaphore_signal(barrier, inc=1, device_id=z_peer(dz), device_id_type=MESH)

    small[0].wait()
    n_t = NZL * NY * NC
    own = lax.broadcasted_iota(jnp.int32, (n_t, n_t), 0) == lax.broadcasted_iota(jnp.int32, (n_t, n_t), 1)
    column = jnp.sum(jnp.where(own, weight_ref[...], 0.0), axis=1, keepdims=True)
    w_rows[...] = jnp.broadcast_to(column, (n_t, HALF)).reshape(NZL, NY * NC, HALF)

    def product(n, value):
        rows = slice(n * ROWS, (n + 1) * ROWS)
        p_high[rows, :], p_low[rows, :] = two_halves(value)
        both = dot(v_t[:, rows], p_high[rows, :])
        return both[:MODES] + both[MODES:] + dot(v_t[:MODES, rows], p_low[rows, :])

    def keep_q(chunk, c, q):
        qt = q.T
        for y_ in range(NY):
            for c_ in range(NC):
                for h in range(2):
                    lanes = slice(h * HALF, (h + 1) * HALF)
                    row = (y_ * NC + c_) * BLOCK
                    qx_buf[chunk, c * 2 + h, y_ * NC + c_] = qt[row : row + BLOCK, lanes]
                    row += HALF
                    qy_buf[chunk, y_ * NC + c_, c * 2 + h] = qt[row : row + BLOCK, lanes]

    def project(chunk):
        lanes = slice(chunk * MODES, (chunk + 1) * MODES)
        if chunk == 0:
            load_v[0].wait()
            v_real = v_buf[0].T
            keep_v(0, v_real)
        load_p[chunk][0].wait()
        rr = product(0, p_buf[0, :, lanes])
        if chunk == 0:
            load_v[1].wait()
            v_imag = v_buf[1].T
            keep_v(1, v_imag)
            keep_v(2, v_real - v_imag)
        load_p[chunk][1].wait()
        ii = product(1, p_buf[1, :, lanes])
        keep_q(chunk, 0, rr + ii)
        keep_q(chunk, 1, product(2, p_buf[0, :, lanes] + p_buf[1, :, lanes]) - rr + ii)

    def send(src, dst, send_sem, recv_sem, to):
        pltpu.make_async_remote_copy(
            src_ref=src, dst_ref=dst, send_sem=send_sem, recv_sem=recv_sem, device_id=to, device_id_type=MESH
        ).start()

    def yc_index(dy, dc):
        return lax.rem(y + dy, NY) * NC + lax.rem(core + dc, NC)

    def arrived(ref, sem):
        pltpu.make_async_copy(ref, ref, sem).wait()

    def scatter(chunk):
        for n in range(len(YC_PEERS)):
            dy, dc = YC_PEERS[n]
            send(qy_buf.at[chunk, yc_index(dy, dc)], y1.at[chunk, n], send_sem.at[1], y1_recv.at[chunk], yc_peer(dy, dc))
            if n < len(X_PEERS):
                dx = X_PEERS[n]
                send(qx_buf.at[chunk, lax.rem(x + dx, NX)], x1.at[chunk, n], send_sem.at[0], x1_recv.at[chunk], x_peer(dx))

    def weighted(zlp, own, others):
        total = own * w_got[zlp, pl.ds(y * NC + core, 1), :]
        for n, (dy, dc) in enumerate(YC_PEERS):
            source = lax.rem(y + NY - dy, NY) * NC + lax.rem(core + dc, NC)
            total = total + others[n] * w_got[zlp, pl.ds(source, 1), :]
        return total

    def across(chunk):
        arrived(x1.at[chunk], x1_recv.at[chunk])
        total = qx_buf[chunk, x]
        for n in range(len(X_PEERS)):
            total = total + x1[chunk, n]
        x_sum[chunk] = total
        for n, (dy, dc) in enumerate(YC_PEERS):
            send(x_sum.at[chunk, yc_index(dy, dc)], y2.at[chunk, n], send_sem.at[2], y2_recv.at[chunk], yc_peer(dy, dc))
        arrived(y1.at[chunk], y1_recv.at[chunk])
        zlp = CHUNK_ZL[chunk][1]
        for x_ in range(NX):
            y_sum[chunk, x_] = weighted(
                zlp, qy_buf[chunk, y * NC + core, x_], [y1[chunk, n, x_] for n in range(len(YC_PEERS))]
            )
        for n, dx in enumerate(X_PEERS):
            send(y_sum.at[chunk, lax.rem(x + dx, NX)], x2.at[chunk, n], send_sem.at[3], x2_recv.at[chunk], x_peer(dx))

    def along_z(chunk, i):
        zlp, at = CHUNK_ZL[chunk][i], chunk * 2 + i
        if i == 0:
            arrived(y2.at[chunk], y2_recv.at[chunk])
            total = weighted(zlp, x_sum[chunk, y * NC + core], [y2[chunk, n] for n in range(len(YC_PEERS))])
        else:
            arrived(x2.at[chunk], x2_recv.at[chunk])
            total = y_sum[chunk, x]
            for n in range(len(X_PEERS)):
                total = total + x2[chunk, n]
        s1_sum[at] = total

    def to_z(at, zh_):
        zlp = CHUNK_ZL[at // 2][at % 2]
        here = z == zh_ * NZL + zlp

        @pl.when(jnp.logical_not(here))
        def _():
            send(s1_sum.at[at], s2.at[z], send_sem.at[4], s2_recv, device(x, y, zh_, zlp, core))

        @pl.when(here)
        def _():
            s2[z] = s1_sum[at]

    project(0)
    pl.semaphore_wait(barrier, len(X_PEERS) + len(YC_PEERS) + z)
    for dz in range(1, NZL):

        @pl.when(dz <= zl)
        def _():
            pl.semaphore_signal(near_sem, inc=1, device_id=z_peer(-dz), device_id_type=MESH)
            send(w_rows.at[zl - dz], w_got.at[zl], send_sem.at[5], w_recv, z_peer(-dz))

    scatter(0)
    project(1)
    scatter(1)

    for dz in range(1, N_Z):

        @pl.when((dz > zl) & (dz <= z))
        def _():
            pl.semaphore_signal(far_sem, inc=1, device_id=z_peer(-dz), device_id_type=MESH)

    w_got[zl] = w_rows[zl]

    @pl.when(zl < NZL - 1)
    def _():
        pl.semaphore_wait(near_sem, NZL - 1 - zl)

    for dz in range(1, NZL):

        @pl.when(zl + dz < NZL)
        def _():
            send(w_rows.at[zl + dz], w_got.at[zl], send_sem.at[5], w_recv, z_peer(dz))


    for load in small[1:]:
        load.wait()
    er, ei = noise_ref[0], noise_ref[1]
    qr, qi = probe_ref[0], probe_ref[1]
    prod_real = er * qr + ei * qi
    prod_imag = er * qi - ei * qr
    lace_of = lax.rem(lax.broadcasted_iota(jnp.int32, (4, MODES), 1), LACE_CLASSES)
    spin_of = lax.broadcasted_iota(jnp.int32, (4, 1), 0)
    row = lax.broadcasted_iota(jnp.int32, (16, 16), 0)
    col = lax.broadcasted_iota(jnp.int32, (16, 16), 1)
    m_real = jnp.zeros((16, 16), F32)
    m_imag = jnp.zeros((16, 16), F32)
    for k in range(4):
        lace = (lace_of == lace_ref[0, k]).astype(F32)
        spin = (spin_of == spin_ref[0, k]).astype(F32)
        wr = jnp.sum(prod_real * lace, axis=1, keepdims=True) * spin
        wi = jnp.sum(prod_imag * lace, axis=1, keepdims=True) * spin
        here = (lax.div(col, 4) == k) & (lax.rem(col, 4) == lax.div(row, 4))
        m_real += jnp.where(here, jnp.concatenate([wr] * 4, axis=0), 0.0)
        m_imag += jnp.where(here, jnp.concatenate([wi] * 4, axis=0), 0.0)
    mix = jnp.concatenate(
        [jnp.concatenate([m_real, -m_imag], axis=1), jnp.concatenate([m_imag, m_real], axis=1)], axis=0
    )

    arrived(w_got.at[pl.ds(0, 3)], w_recv)
    across(0)
    across(1)

    @pl.when(zh < NZH - 1)
    def _():
        pl.semaphore_wait(far_sem, (NZH - 1 - zh) * NZL)

    for chunk in range(2):
        for i in range(2):
            along_z(chunk, i)
            to_z(chunk * 2 + i, 0)
        for at in range(chunk * 2, chunk * 2 + 2):
            to_z(at, 1)
    for zh_ in range(2, NZH):
        for at in range(4):
            to_z(at, zh_)

    n_z = NZH * NZL - 1
    arrived(s2.at[pl.ds(0, n_z)], s2_recv)
    total = s2[0]
    for n in range(1, n_z + 1):
        total = total + s2[n]
    y_all[x] = total
    for dx in X_PEERS:
        send(y_all.at[x], y_all.at[x], send_sem.at[6], y_recv, x_peer(dx))
    arrived(y_all.at[pl.ds(0, 3)], y_recv)

    y_cat = jnp.concatenate(
        [
            jnp.concatenate([y_all[0], y_all[1]], axis=1),
            jnp.concatenate([y_all[2], y_all[3]], axis=1),
        ],
        axis=0,
    )
    z_cat = lax.dot_general(
        mix, y_cat, (((1,), (0,)), ((), ())), precision=lax.Precision.HIGHEST, preferred_element_type=F32
    )
    z_high, z_low = two_halves(z_cat)
    z_both = jnp.concatenate([z_high, z_low], axis=0)
    leaving = []
    for third in range(ROWS // MODES):
        f = []
        for n in range(2):
            rows = slice(n * ROWS + third * MODES, n * ROWS + (third + 1) * MODES)
            both = dot(z_both, v_t[:MODES, rows])
            f.append(both[:32] + both[32:] + dot(z_high, v_t[MODES:, rows]))
        out_buf[third, 0] = f[0][:16] - f[1][16:]
        out_buf[third, 1] = f[0][16:] + f[1][:16]
        copy = pltpu.make_async_copy(
            out_buf.at[third], out_ref.at[0, :, :, pl.ds(third * MODES, MODES)], out_sem.at[third]
        )
        copy.start()
        leaving.append(copy)

    for n, ref in enumerate(
        (x1, y1, y2, x2, s2.at[pl.ds(0, n_z)], w_got.at[pl.ds(0, 3)], y_all.at[pl.ds(0, 3)])
    ):
        arrived(ref, send_sem.at[n])
    for copy in leaving:
        copy.wait()


def per_device(evecs, solutions, weights, noise, probe, spin, lace):
    hbm = pl.BlockSpec(memory_space=pltpu.HBM)
    dma = pltpu.SemaphoreType.DMA
    return pl.pallas_call(
        kernel,
        out_shape=jax.ShapeDtypeStruct((1, 2, BLOCK, ROWS), F32),
        in_specs=[hbm] * 7,
        out_specs=hbm,
        scratch_shapes=[
            pltpu.VMEM((1, NZL * NY * NC), F32),
            pltpu.VMEM((2, 4, MODES), F32),
            pltpu.VMEM((2, 4, MODES), F32),
            pltpu.SMEM((1, 4), jnp.int32),
            pltpu.SMEM((1, 4), jnp.int32),
            pltpu.VMEM((2, ROWS, MODES), F32),
            pltpu.VMEM((2, ROWS, 2 * MODES), F32),
            pltpu.VMEM((2 * MODES, 3 * ROWS), BF16),
            pltpu.VMEM((3 * ROWS, MODES), BF16),
            pltpu.VMEM((3 * ROWS, MODES), BF16),
            pltpu.VMEM((2, NX, NY * NC, BLOCK, HALF), F32),
            pltpu.VMEM((2, NY * NC, NX, BLOCK, HALF), F32),
            pltpu.VMEM((2, len(X_PEERS), NY * NC, BLOCK, HALF), F32),
            pltpu.VMEM((2, len(YC_PEERS), NX, BLOCK, HALF), F32),
            pltpu.VMEM((2, NY * NC, BLOCK, HALF), F32),
            pltpu.VMEM((2, NX, BLOCK, HALF), F32),
            pltpu.VMEM((2, len(YC_PEERS), BLOCK, HALF), F32),
            pltpu.VMEM((2, len(X_PEERS), BLOCK, HALF), F32),
            pltpu.VMEM((4, BLOCK, HALF), F32),
            pltpu.VMEM((NZH * NZL, BLOCK, HALF), F32),
            pltpu.VMEM((4, BLOCK, HALF), F32),
            pltpu.VMEM((NZL, NY * NC, HALF), F32),
            pltpu.VMEM((NZL, NY * NC, HALF), F32),
            dma((6,)), dma((5,)), dma, dma((2,)), dma((2,)), dma((2,)), dma((2,)), dma, dma, dma((7,)),
            pltpu.SemaphoreType.REGULAR, pltpu.SemaphoreType.REGULAR,
            pltpu.VMEM((ROWS // MODES, 2, BLOCK, MODES), F32), dma((ROWS // MODES,)),
        ],
        compiler_params=pltpu.CompilerParams(
            collective_id=0, has_side_effects=True, vmem_limit_bytes=62 * 2**20
        ),
        cost_estimate=pl.CostEstimate(flops=2_500_000_000, bytes_accessed=4_900_000, transcendentals=0),
    )(evecs, solutions, weights.T, noise, probe, spin, lace)


def solution(mesh):
    placed = (
        P("tm", None, "space", None),
        P("tm", None, "space", None),
        P(None, "tm"),
        P("tm", None, None, None),
        P("tm", None, None, None),
        P("tm", None),
        P("tm", None),
    )
    return jax.shard_map(
        per_device,
        mesh=mesh,
        in_specs=placed,
        out_specs=P("tm", None, None, "space"),
        check_vma=False,
    )
```

```python
import jax
import jax.numpy as jnp
from jax import lax
from jax.experimental import pallas as pl
from jax.experimental.pallas import tpu as pltpu
from jax.sharding import PartitionSpec as P

F32 = jnp.float32
BF16 = jnp.bfloat16
MESH = pl.DeviceIdType.MESH

NX, NY, NC, NZH, NZL = 4, 4, 2, 4, 4
MODES = 256
HALF = 128
ROWS = 768
BLOCK = 16
LACE_CLASSES = 8


def ring(d, n):
    return min(d, n - d)


CHUNK_ZL = ((0, 1), (2, 3))
X_PEERS = sorted(range(1, NX), key=lambda d: -ring(d, NX))
YC_PEERS = sorted(
    [(dy, dc) for dy in range(NY) for dc in range(NC) if (dy, dc) != (0, 0)], key=lambda o: -ring(o[0], NY)
)
N_Z = NZH * NZL
FIRST_ZH, LAST_ZH = (0, 1), (2, 3)


def two_halves(value):
    high = value.astype(BF16)
    return high, (value - high.astype(F32)).astype(BF16)


def dot(left, right):
    return lax.dot_general(left, right, (((1,), (0,)), ((), ())), preferred_element_type=F32)


def kernel(
    v_hbm, p_hbm, weight_hbm, noise_hbm, probe_hbm, spin_hbm, lace_hbm,
    out_ref,
    weight_ref, noise_ref, probe_ref, spin_ref, lace_ref,
    v_buf, p_buf, v_t, p_high, p_low, qx_buf, qy_buf,
    x1, y1, x_sum, y_sum, y2, x2, s1_sum, s2, y_all, w_rows, w_got,
    load_sem, small_sem, w_recv, x1_recv, y1_recv, y2_recv, x2_recv, s2_recv, y_recv, send_sem, near_sem, far_sem,
):
    t = lax.axis_index("tm")
    s = lax.axis_index("space")
    core = lax.rem(t, NC)
    y = lax.rem(t // NC, NY)
    zl = t // (NC * NY)
    x = s // NZH
    zh = lax.rem(s, NZH)

    def device(x_, y_, zh_, zl_, c_):
        return ((zl_ * NY + y_) * NC + c_, x_ * NZH + zh_)

    z = zh * NZL + zl

    def z_peer(dz):
        z_ = z + dz
        return device(x, y, z_ // NZL, lax.rem(z_, NZL), core)

    def x_peer(dx):
        return device(lax.rem(x + dx, NX), y, zh, zl, core)

    def yc_peer(dy, dc):
        return device(x, lax.rem(y + dy, NY), zh, zl, lax.rem(core + dc, NC))

    small = []
    for n, (hbm, ref) in enumerate(
        (
            (weight_hbm, weight_ref),
            (noise_hbm.at[0], noise_ref),
            (probe_hbm.at[0], probe_ref),
            (spin_hbm, spin_ref),
            (lace_hbm, lace_ref),
        )
    ):
        small.append(pltpu.make_async_copy(hbm, ref, small_sem.at[n]))
    load_v = [pltpu.make_async_copy(v_hbm.at[0, c], v_buf.at[c], load_sem.at[c]) for c in range(2)]
    load_p = [
        [
            pltpu.make_async_copy(
                p_hbm.at[0, c, :, pl.ds(chunk * MODES, MODES)],
                p_buf.at[c, :, pl.ds(chunk * MODES, MODES)],
                load_sem.at[2 + chunk * 2 + c],
            )
            for c in range(2)
        ]
        for chunk in range(2)
    ]
    for c in range(2):
        load_v[c].start()
        load_p[0][c].start()
    barrier = pltpu.get_barrier_semaphore()
    for dx in X_PEERS:
        pl.semaphore_signal(barrier, inc=1, device_id=x_peer(dx), device_id_type=MESH)
    for dy, dc in YC_PEERS:
        pl.semaphore_signal(barrier, inc=1, device_id=yc_peer(dy, dc), device_id_type=MESH)
    for c in range(2):
        load_p[1][c].start()
    for load in small:
        load.start()

    def keep_v(n, value):
        rows = slice(n * ROWS, (n + 1) * ROWS)
        v_t[:MODES, rows], v_t[MODES:, rows] = two_halves(value)

    for dz in range(1, N_Z):

        @pl.when(z + dz < N_Z)
        def _():
            pl.semaphore_signal(barrier, inc=1, device_id=z_peer(dz), device_id_type=MESH)

    small[0].wait()
    n_t = NZL * NY * NC
    own = lax.broadcasted_iota(jnp.int32, (n_t, n_t), 0) == lax.broadcasted_iota(jnp.int32, (n_t, n_t), 1)
    column = jnp.sum(jnp.where(own, weight_ref[...], 0.0), axis=1, keepdims=True)
    w_rows[...] = jnp.broadcast_to(column, (n_t, HALF)).reshape(NZL, NY * NC, HALF)

    def product(n, value):
        rows = slice(n * ROWS, (n + 1) * ROWS)
        p_high[rows, :], p_low[rows, :] = two_halves(value)
        both = dot(v_t[:, rows], p_high[rows, :])
        return both[:MODES] + both[MODES:] + dot(v_t[:MODES, rows], p_low[rows, :])

    def keep_q(chunk, c, q):
        qt = q.T
        for y_ in range(NY):
            for c_ in range(NC):
                for h in range(2):
                    lanes = slice(h * HALF, (h + 1) * HALF)
                    row = (y_ * NC + c_) * BLOCK
                    qx_buf[chunk, c * 2 + h, y_ * NC + c_] = qt[row : row + BLOCK, lanes]
                    row += HALF
                    qy_buf[chunk, y_ * NC + c_, c * 2 + h] = qt[row : row + BLOCK, lanes]

    def project(chunk):
        lanes = slice(chunk * MODES, (chunk + 1) * MODES)
        if chunk == 0:
            load_v[0].wait()
            v_real = v_buf[0].T
            keep_v(0, v_real)
        load_p[chunk][0].wait()
        rr = product(0, p_buf[0, :, lanes])
        if chunk == 0:
            load_v[1].wait()
            v_imag = v_buf[1].T
            keep_v(1, v_imag)
            keep_v(2, v_real - v_imag)
        load_p[chunk][1].wait()
        ii = product(1, p_buf[1, :, lanes])
        keep_q(chunk, 0, rr + ii)
        keep_q(chunk, 1, product(2, p_buf[0, :, lanes] + p_buf[1, :, lanes]) - rr + ii)

    def send(src, dst, send_sem, recv_sem, to):
        pltpu.make_async_remote_copy(
            src_ref=src, dst_ref=dst, send_sem=send_sem, recv_sem=recv_sem, device_id=to, device_id_type=MESH
        ).start()

    def yc_index(dy, dc):
        return lax.rem(y + dy, NY) * NC + lax.rem(core + dc, NC)

    def arrived(ref, sem):
        pltpu.make_async_copy(ref, ref, sem).wait()

    def scatter(chunk):
        for n in range(len(YC_PEERS)):
            dy, dc = YC_PEERS[n]
            send(qy_buf.at[chunk, yc_index(dy, dc)], y1.at[chunk, n], send_sem.at[1], y1_recv.at[chunk], yc_peer(dy, dc))
            if n < len(X_PEERS):
                dx = X_PEERS[n]
                send(qx_buf.at[chunk, lax.rem(x + dx, NX)], x1.at[chunk, n], send_sem.at[0], x1_recv.at[chunk], x_peer(dx))

    def weighted(zlp, own, others):
        total = own * w_got[zlp, pl.ds(y * NC + core, 1), :]
        for n, (dy, dc) in enumerate(YC_PEERS):
            source = lax.rem(y + NY - dy, NY) * NC + lax.rem(core + dc, NC)
            total = total + others[n] * w_got[zlp, pl.ds(source, 1), :]
        return total

    def across(chunk):
        arrived(x1.at[chunk], x1_recv.at[chunk])
        total = qx_buf[chunk, x]
        for n in range(len(X_PEERS)):
            total = total + x1[chunk, n]
        x_sum[chunk] = total
        for n, (dy, dc) in enumerate(YC_PEERS):
            send(x_sum.at[chunk, yc_index(dy, dc)], y2.at[chunk, n], send_sem.at[2], y2_recv.at[chunk], yc_peer(dy, dc))
        arrived(y1.at[chunk], y1_recv.at[chunk])
        zlp = CHUNK_ZL[chunk][1]
        for x_ in range(NX):
            y_sum[chunk, x_] = weighted(
                zlp, qy_buf[chunk, y * NC + core, x_], [y1[chunk, n, x_] for n in range(len(YC_PEERS))]
            )
        for n, dx in enumerate(X_PEERS):
            send(y_sum.at[chunk, lax.rem(x + dx, NX)], x2.at[chunk, n], send_sem.at[3], x2_recv.at[chunk], x_peer(dx))

    def along_z(chunk, i):
        zlp, at = CHUNK_ZL[chunk][i], chunk * 2 + i
        if i == 0:
            arrived(y2.at[chunk], y2_recv.at[chunk])
            total = weighted(zlp, x_sum[chunk, y * NC + core], [y2[chunk, n] for n in range(len(YC_PEERS))])
        else:
            arrived(x2.at[chunk], x2_recv.at[chunk])
            total = y_sum[chunk, x]
            for n in range(len(X_PEERS)):
                total = total + x2[chunk, n]
        s1_sum[at] = total

    def to_z(at, zh_):
        zlp = CHUNK_ZL[at // 2][at % 2]
        here = z == zh_ * NZL + zlp

        @pl.when(jnp.logical_not(here))
        def _():
            send(s1_sum.at[at], s2.at[z], send_sem.at[4], s2_recv, device(x, y, zh_, zlp, core))

        @pl.when(here)
        def _():
            s2[z] = s1_sum[at]

    project(0)
    pl.semaphore_wait(barrier, len(X_PEERS) + len(YC_PEERS) + z)
    for dz in range(1, NZL):

        @pl.when(dz <= zl)
        def _():
            pl.semaphore_signal(near_sem, inc=1, device_id=z_peer(-dz), device_id_type=MESH)
            send(w_rows.at[zl - dz], w_got.at[zl], send_sem.at[5], w_recv, z_peer(-dz))

    scatter(0)
    project(1)
    scatter(1)

    for dz in range(1, N_Z):

        @pl.when((dz > zl) & (dz <= z))
        def _():
            pl.semaphore_signal(far_sem, inc=1, device_id=z_peer(-dz), device_id_type=MESH)

    w_got[zl] = w_rows[zl]

    @pl.when(zl < NZL - 1)
    def _():
        pl.semaphore_wait(near_sem, NZL - 1 - zl)

    for dz in range(1, NZL):

        @pl.when(zl + dz < NZL)
        def _():
            send(w_rows.at[zl + dz], w_got.at[zl], send_sem.at[5], w_recv, z_peer(dz))


    for load in small[1:]:
        load.wait()
    er, ei = noise_ref[0], noise_ref[1]
    qr, qi = probe_ref[0], probe_ref[1]
    prod_real = er * qr + ei * qi
    prod_imag = er * qi - ei * qr
    lace_of = lax.rem(lax.broadcasted_iota(jnp.int32, (4, MODES), 1), LACE_CLASSES)
    spin_of = lax.broadcasted_iota(jnp.int32, (4, 1), 0)
    row = lax.broadcasted_iota(jnp.int32, (16, 16), 0)
    col = lax.broadcasted_iota(jnp.int32, (16, 16), 1)
    m_real = jnp.zeros((16, 16), F32)
    m_imag = jnp.zeros((16, 16), F32)
    for k in range(4):
        lace = (lace_of == lace_ref[0, k]).astype(F32)
        spin = (spin_of == spin_ref[0, k]).astype(F32)
        wr = jnp.sum(prod_real * lace, axis=1, keepdims=True) * spin
        wi = jnp.sum(prod_imag * lace, axis=1, keepdims=True) * spin
        here = (lax.div(col, 4) == k) & (lax.rem(col, 4) == lax.div(row, 4))
        m_real += jnp.where(here, jnp.concatenate([wr] * 4, axis=0), 0.0)
        m_imag += jnp.where(here, jnp.concatenate([wi] * 4, axis=0), 0.0)
    mix = jnp.concatenate(
        [jnp.concatenate([m_real, -m_imag], axis=1), jnp.concatenate([m_imag, m_real], axis=1)], axis=0
    )

    arrived(w_got.at[pl.ds(0, 3)], w_recv)
    across(0)
    across(1)

    @pl.when(zh < NZH - 1)
    def _():
        pl.semaphore_wait(far_sem, (NZH - 1 - zh) * NZL)

    for chunk in range(2):
        for i in range(2):
            along_z(chunk, i)
            to_z(chunk * 2 + i, 0)
        for at in range(chunk * 2, chunk * 2 + 2):
            to_z(at, 1)
    for zh_ in range(2, NZH):
        for at in range(4):
            to_z(at, zh_)

    n_z = NZH * NZL - 1
    arrived(s2.at[pl.ds(0, n_z)], s2_recv)
    total = s2[0]
    for n in range(1, n_z + 1):
        total = total + s2[n]
    y_all[x] = total
    for dx in X_PEERS:
        send(y_all.at[x], y_all.at[x], send_sem.at[6], y_recv, x_peer(dx))
    arrived(y_all.at[pl.ds(0, 3)], y_recv)

    y_cat = jnp.concatenate(
        [
            jnp.concatenate([y_all[0], y_all[1]], axis=1),
            jnp.concatenate([y_all[2], y_all[3]], axis=1),
        ],
        axis=0,
    )
    z_cat = lax.dot_general(
        mix, y_cat, (((1,), (0,)), ((), ())), precision=lax.Precision.HIGHEST, preferred_element_type=F32
    )
    z_high, z_low = two_halves(z_cat)
    z_both = jnp.concatenate([z_high, z_low], axis=0)
    f = []
    for n in range(2):
        rows = slice(n * ROWS, (n + 1) * ROWS)
        both = dot(z_both, v_t[:MODES, rows])
        f.append(both[:32] + both[32:] + dot(z_high, v_t[MODES:, rows]))
    out_ref[0, 0] = f[0][:16] - f[1][16:]
    out_ref[0, 1] = f[0][16:] + f[1][:16]

    for n, ref in enumerate(
        (x1, y1, y2, x2, s2.at[pl.ds(0, n_z)], w_got.at[pl.ds(0, 3)], y_all.at[pl.ds(0, 3)])
    ):
        arrived(ref, send_sem.at[n])


def per_device(evecs, solutions, weights, noise, probe, spin, lace):
    vmem = pl.BlockSpec(memory_space=pltpu.VMEM)
    hbm = pl.BlockSpec(memory_space=pltpu.HBM)
    dma = pltpu.SemaphoreType.DMA
    return pl.pallas_call(
        kernel,
        out_shape=jax.ShapeDtypeStruct((1, 2, BLOCK, ROWS), F32),
        in_specs=[hbm] * 7,
        out_specs=vmem,
        scratch_shapes=[
            pltpu.VMEM((1, NZL * NY * NC), F32),
            pltpu.VMEM((2, 4, MODES), F32),
            pltpu.VMEM((2, 4, MODES), F32),
            pltpu.SMEM((1, 4), jnp.int32),
            pltpu.SMEM((1, 4), jnp.int32),
            pltpu.VMEM((2, ROWS, MODES), F32),
            pltpu.VMEM((2, ROWS, 2 * MODES), F32),
            pltpu.VMEM((2 * MODES, 3 * ROWS), BF16),
            pltpu.VMEM((3 * ROWS, MODES), BF16),
            pltpu.VMEM((3 * ROWS, MODES), BF16),
            pltpu.VMEM((2, NX, NY * NC, BLOCK, HALF), F32),
            pltpu.VMEM((2, NY * NC, NX, BLOCK, HALF), F32),
            pltpu.VMEM((2, len(X_PEERS), NY * NC, BLOCK, HALF), F32),
            pltpu.VMEM((2, len(YC_PEERS), NX, BLOCK, HALF), F32),
            pltpu.VMEM((2, NY * NC, BLOCK, HALF), F32),
            pltpu.VMEM((2, NX, BLOCK, HALF), F32),
            pltpu.VMEM((2, len(YC_PEERS), BLOCK, HALF), F32),
            pltpu.VMEM((2, len(X_PEERS), BLOCK, HALF), F32),
            pltpu.VMEM((4, BLOCK, HALF), F32),
            pltpu.VMEM((NZH * NZL, BLOCK, HALF), F32),
            pltpu.VMEM((4, BLOCK, HALF), F32),
            pltpu.VMEM((NZL, NY * NC, HALF), F32),
            pltpu.VMEM((NZL, NY * NC, HALF), F32),
            dma((6,)), dma((5,)), dma, dma((2,)), dma((2,)), dma((2,)), dma((2,)), dma, dma, dma((7,)),
            pltpu.SemaphoreType.REGULAR, pltpu.SemaphoreType.REGULAR,
        ],
        compiler_params=pltpu.CompilerParams(
            collective_id=0, has_side_effects=True, vmem_limit_bytes=62 * 2**20
        ),
        cost_estimate=pl.CostEstimate(flops=2_500_000_000, bytes_accessed=4_900_000, transcendentals=0),
    )(evecs, solutions, weights.T, noise, probe, spin, lace)


def solution(mesh):
    placed = (
        P("tm", None, "space", None),
        P("tm", None, "space", None),
        P(None, "tm"),
        P("tm", None, None, None),
        P("tm", None, None, None),
        P("tm", None),
        P("tm", None),
    )
    return jax.shard_map(
        per_device,
        mesh=mesh,
        in_specs=placed,
        out_specs=P("tm", None, None, "space"),
        check_vma=False,
    )
```
